32 devices in a mesh: slab: 16 (over z, x, core), col: 2 (over y).
Axes of the slice: x: 2, y: 2, z: 4, core: 2. Of those that a mesh axis runs over, the one named last changes fastest.
Arguments:
- green_blocks: float32 [16, 2, 2048, 2048], P('slab', None, None, 'col'), may hold values from -0.125 to 0.125
- traces: float32 [16, 2, 64, 2048], P('slab', None, None, 'col'), may hold values from -6 to 6
- sources: float32 [16, 2, 64, 2048], P('slab', None, None, 'col'), may hold values from -6 to 6
Outputs:
- swept: float32 [16, 2, 64, 2048], P('slab', None, None, 'col')
The draws below stay inside these ranges and needn't reach their ends.
All inputs are finite; a program needn't handle non-finite values.
Results may differ from the reference program's by a relative error of at most 0.00014.
Values sent between devices are 32-bit elements; how exact they have to be, the bound alone decides.
No kernel may reach another device: no remote copies, remote signals or barrier semaphores. Data moves between devices by JAX's collectives and lax.ppermute only.
A program may use at most 64 MiB of HBM per device.

```python
import jax
import jax.numpy as jnp
from jax import lax

C = 2048
SHOTS = 64
STEPS = 4
SLABS = 16


def strengthened(array, rng, source, target, blocks, factor):
    def block_of(dim):
        return (jnp.arange(array.shape[dim]) // (array.shape[dim] // blocks)).reshape((-1,) + (1,) * (array.ndim - 1 - dim))

    near = jax.random.permutation(rng, blocks)[block_of(target)]
    second = (block_of(target) + blocks // 2) % blocks
    return jnp.where((block_of(source) == near) | (block_of(source) == second), factor * array, array)


def steps_of(key, extent, pieces, smallest, top_value):
    def one(position, shards_of):
        heights = jax.random.uniform(jax.random.fold_in(jax.random.fold_in(key, 6), position), (shards_of,), jnp.float32, smallest / len(pieces), top_value / len(pieces))
        return jnp.repeat(jnp.exp(heights), extent[position] // shards_of).reshape((-1,) + (1,) * (len(extent) - position - 1))

    level = one(*pieces[0])
    for cut in pieces[1:]:
        level = level * one(*cut)
    return level


def centred(rng, shape, deviation, limit, pieces=(), held_as=jnp.bfloat16):
    drawn = jax.random.normal(rng, shape, jnp.float32) * deviation
    if len(pieces) > 0:
        drawn = steps_of(rng, shape, pieces, -0.22, 0.18) * drawn
    return jnp.clip(drawn, min=-limit, max=limit).astype(held_as)


def noise_with(rng, dims, width, reach, cuts, heavy, dtype=jnp.bfloat16):
    values = width * jax.random.normal(rng, dims, jnp.float32)
    if cuts:
        values = values * steps_of(rng, dims, cuts, -0.22, 0.18)
    return jnp.clip(strengthened(values, jax.random.fold_in(rng, 3), *heavy), -reach, reach).astype(dtype)


def setup_inputs(seed: int = 0) -> dict:
    arg_keys = jax.random.split(jax.random.key(seed), 4)
    green_blocks = noise_with(arg_keys[0], (SLABS, 2, C, C), (2 * C) ** -0.5, 0.125, ((0, 16), (3, 2)), (3, 2, 2, 2.0), jnp.float32)
    traces = centred(arg_keys[1], (SLABS, 2, SHOTS, C), 1.0, 6.0, ((0, 16), (3, 2)), jnp.float32)
    sources = centred(arg_keys[2], (SLABS, 2, SHOTS, C), 1.0, 6.0, ((0, 16), (3, 2)), jnp.float32)
    return dict(green_blocks=green_blocks, traces=traces, sources=sources)


def matmul_t(left, right):
    return lax.dot_general(left, right, (((1,), (1,)), ((), ())), precision=lax.Precision.HIGHEST, preferred_element_type=jnp.float32)


def one_slab(packed):
    matrix, incoming, own_source = packed
    real_out = matmul_t(incoming[0], matrix[0]) - matmul_t(incoming[1], matrix[1]) + own_source[0]
    imag_out = matmul_t(incoming[1], matrix[0]) + matmul_t(incoming[0], matrix[1]) + own_source[1]
    return jnp.stack([real_out, imag_out], 0)


def reference(green_blocks, traces, sources):
    current = traces
    for step_index in range(STEPS):
        from_above = jnp.concatenate([jnp.zeros_like(current[:1]), current[:-1]], 0)
        current = lax.map(one_slab, (green_blocks, from_above, sources))
    return current
```

```python
import functools

import jax
import jax.numpy as jnp
from jax import lax
from jax.experimental import pallas as pl
from jax.experimental.pallas import tpu as pltpu
from jax.sharding import PartitionSpec as P

STEPS = 4
ROWS = 256
BUFFERS = 3
VMEM_LIMIT = 20 << 20
FIRST = (1, 1, 1, 1)

f32 = jnp.float32
bf16 = jnp.bfloat16


def in_vmem():
    return pl.BlockSpec(memory_space=pltpu.VMEM)


def pinned(array):
    return pltpu.with_memory_space_constraint(array, pltpu.VMEM)


def call(kernel, args, outs, scratch=(), anywhere=(), flops=0):
    specs = [pl.BlockSpec(memory_space=pl.ANY) if i in anywhere else in_vmem() for i in range(len(args))]
    held = [a if i in anywhere else pinned(a) for i, a in enumerate(args)]
    return pl.pallas_call(
        kernel,
        in_specs=specs,
        out_specs=[in_vmem()] * len(outs),
        out_shape=[pltpu.VMEM(shape, dtype) for shape, dtype in outs],
        scratch_shapes=list(scratch),
        compiler_params=pltpu.CompilerParams(vmem_limit_bytes=VMEM_LIMIT),
        cost_estimate=pl.CostEstimate(flops=flops, bytes_accessed=1 << 20, transcendentals=0),
    )(*held)


def halves(value):
    high = value.astype(bf16)
    return high, (value - high.astype(f32)).astype(bf16)


def split_kernel(green, source, high, low, source_t, buffer, sem):
    rows, depth = green.shape[2], green.shape[3]
    count = rows // ROWS

    def copy(i):
        slot = i % BUFFERS
        return pltpu.make_async_copy(green.at[0, :, pl.ds(i * ROWS, ROWS), :], buffer.at[slot], sem.at[slot])

    for i in range(min(BUFFERS - 1, count)):
        copy(i).start()
    source_t[...] = source[0].reshape(-1, depth).T
    for i in range(count):
        if i + BUFFERS - 1 < count:
            copy(i + BUFFERS - 1).start()
        copy(i).wait()
        for part in range(2):
            value = buffer[i % BUFFERS, part]
            at = (pl.ds(i * ROWS, ROWS), pl.ds(part * depth, depth))
            high[at], low[at] = halves(value)


def split(green, sources):
    _, _, rows, depth = green.shape
    lanes = 2 * sources.shape[2]
    return call(
        split_kernel,
        (green, sources),
        [((rows, 2 * depth), bf16), ((rows, 2 * depth), bf16), ((depth, lanes), f32)],
        [pltpu.VMEM((BUFFERS, 2, ROWS, depth), f32), pltpu.SemaphoreType.DMA((BUFFERS,))],
        anywhere=(0,),
    )


def product(high, low, packed, rows):
    lanes = packed.shape[1] // 2
    both = jnp.dot(high[rows, :], packed[...], preferred_element_type=f32)
    rest = jnp.dot(low[rows, :], packed[:, :lanes], preferred_element_type=f32)
    return both[:, :lanes] + both[:, lanes:] + rest


def rows_of(owner, depth):
    return pl.ds(pl.multiple_of(owner * depth, depth), depth)


def active(parity):
    return lax.rem(lax.axis_index("slab"), 2) == parity


def cross_kernel(parity, raw, n, high, low, *refs):
    incoming, packed, outs = refs[: len(refs) - n], refs[len(refs) - n], refs[len(refs) - n + 1 :]
    depth, lanes = packed.shape[0] // 2, packed.shape[1] // 2
    me = lax.axis_index("col")

    @pl.when(active(parity))
    def _():
        if raw:
            value = incoming[0][0].reshape(lanes, depth).T
        else:
            value = incoming[0][...]
            for ref in incoming[1:]:
                value = value + ref[...]
        turned = pltpu.roll(value, lanes // 2, 1)
        lane = lax.broadcasted_iota(jnp.int32, value.shape, 1)
        turned = jnp.where(lane < lanes // 2, -turned, turned)
        packed[:depth, :lanes], packed[:depth, lanes:] = halves(value)
        packed[depth:, :lanes], packed[depth:, lanes:] = halves(turned)
        for k, out in enumerate(outs):
            out[...] = product(high, low, packed, rows_of(lax.rem(me + k + 1, n), depth))


def own_kernel(parity, n, high, low, packed, source_t, out):
    depth = packed.shape[0] // 2

    @pl.when(active(parity))
    def _():
        out[...] = product(high, low, packed, rows_of(lax.axis_index("col"), depth)) + source_t[...]


def finish_kernel(n, *refs):
    ins, out = refs[:-1], refs[-1]
    for parity in range(2):

        @pl.when(active(parity))
        def _():
            value = ins[parity * n][...]
            for k in range(1, n):
                value = value + ins[parity * n + k][...]
            out[0] = value.T.reshape(out.shape[1:])


def send(value, parity, slabs_on, cols_on):
    slabs, n = lax.axis_size("slab"), lax.axis_size("col")
    route = [
        (s * n + c, (s + slabs_on) * n + (c + cols_on) % n)
        for s in range(parity, slabs - slabs_on, 2)
        for c in range(n)
    ]
    return lax.ppermute(value, ("slab", "col"), route)


def shards(green_blocks, traces, sources):
    n = lax.axis_size("col")
    _, _, shots, depth = traces.shape
    rows, lanes = green_blocks.shape[2], 2 * shots
    flops = 2 * rows * 2 * depth * 3 * lanes
    shifted = {parity: [send(traces, 1 - parity, 1, 0)] for parity in (1, 0)}
    high, low, source_t = split(green_blocks, sources)
    ends = {}
    incoming = {chain: shifted[chain] for chain in (0, 1)}
    for step in range(STEPS):
        last = step == STEPS - 1
        for chain in (FIRST[step], 1 - FIRST[step]):
            parity = (chain + step) % 2
            got = call(
                functools.partial(cross_kernel, parity, step == 0, n),
                (high, low, *incoming[chain]),
                [((2 * depth, 2 * lanes), bf16)] + [((depth, lanes), f32)] * (n - 1),
                flops=flops * (n - 1) // n,
            )
            packed, crossing = got[0], got[1:]
            on = 0 if last else 1
            arriving = [send(value, parity, on, k + 1) for k, value in enumerate(crossing)]
            own = call(
                functools.partial(own_kernel, parity, n),
                (high, low, packed, source_t),
                [((depth, lanes), f32)],
                flops=flops // n,
            )[0]
            if last:
                ends[parity] = [own] + arriving
            else:
                incoming[chain] = arriving + [send(own, parity, 1, 0)]
    return pl.pallas_call(
        functools.partial(finish_kernel, n),
        in_specs=[in_vmem()] * (2 * n),
        out_specs=in_vmem(),
        out_shape=jax.ShapeDtypeStruct(sources.shape, f32),
        compiler_params=pltpu.CompilerParams(vmem_limit_bytes=VMEM_LIMIT),
    )(*[pinned(a) for a in ends[0] + ends[1]])


def solution(mesh):
    placed = P("slab", None, None, "col")
    return jax.shard_map(shards, mesh=mesh, in_specs=(placed,) * 3, out_specs=placed, check_vma=False)
```

```python
import functools

import jax
import jax.numpy as jnp
from jax import lax
from jax.experimental import pallas as pl
from jax.experimental.pallas import tpu as pltpu
from jax.sharding import PartitionSpec as P

STEPS = 4
ROWS = 256
BUFFERS = 3
ORDER = (
    (("open", 1, "cross"), ("open", 1, "own"), ("make", 0, "cross"), ("make", 0, "own"),),
    (("hand", 1, "cross"), ("make", 1, "cross"), ("make", 1, "own"), ("hand", 0, "cross"), ("make", 0, "cross"), ("make", 0, "own"),),
    (("hand", 1, "cross"), ("make", 1, "cross"), ("make", 1, "own"), ("hand", 0, "cross"), ("make", 0, "cross"), ("make", 0, "own"),),
    (("hand", 1, "cross"), ("hand", 0, "cross"),),
)
VMEM_LIMIT = 20 << 20

f32 = jnp.float32
bf16 = jnp.bfloat16


def in_vmem():
    return pl.BlockSpec(memory_space=pltpu.VMEM)


def pinned(array):
    return pltpu.with_memory_space_constraint(array, pltpu.VMEM)


def call(kernel, args, outs, scratch=(), far=(), after=(), cost=0, **more):
    held = [pltpu.with_memory_space_constraint(a, pltpu.HBM) for a in far] + [pinned(a) for a in args]
    specs = [pl.BlockSpec(memory_space=pltpu.HBM)] * len(far) + [in_vmem()] * len(args)
    first, skip = len(held), len(after)

    def body(*refs):
        kernel(*refs[:first], *refs[first + skip :])

    return pl.pallas_call(
        body,
        in_specs=specs + [pl.BlockSpec(memory_space=pl.ANY)] * skip,
        out_specs=[in_vmem()] * len(outs),
        out_shape=[pltpu.VMEM(shape, dtype) for shape, dtype in outs],
        scratch_shapes=list(scratch),
        compiler_params=pltpu.CompilerParams(vmem_limit_bytes=VMEM_LIMIT),
        cost_estimate=pl.CostEstimate(flops=cost, bytes_accessed=0, transcendentals=0),
        **more,
    )(*held, *after)


def halves(value):
    high = value.astype(bf16)
    return high, (value - high.astype(f32)).astype(bf16)


def pass_kernel(value, out):
    pass


def product(high, low, packed, rows):
    lanes = packed.shape[1] // 2
    both = jnp.dot(high[rows, :], packed[...], preferred_element_type=f32)
    rest = jnp.dot(low[rows, :], packed[:, :lanes], preferred_element_type=f32)
    return both[:, :lanes] + both[:, lanes:] + rest


def active(parity):
    return lax.rem(lax.axis_index("slab"), 2) == parity


def fill(packed, incoming, raw):
    depth, lanes = packed.shape[0] // 2, packed.shape[1] // 2
    if raw:
        value = incoming[0][0].reshape(lanes, depth).T
    else:
        value = incoming[0][...]
        for ref in incoming[1:]:
            value = value + ref[...]
    turned = pltpu.roll(value, lanes // 2, 1)
    lane = lax.broadcasted_iota(jnp.int32, value.shape, 1)
    turned = jnp.where(lane < lanes // 2, -turned, turned)
    packed[:depth, :lanes], packed[:depth, lanes:] = halves(value)
    packed[depth:, :lanes], packed[depth:, lanes:] = halves(turned)


def opening_kernel(parity, part, n, green, *refs):
    cross = part == "cross"
    outs = n - 1 if cross else 1
    buffer, sem = refs[-2:]
    refs, outs = refs[: -2 - outs], refs[-2 - outs : -2]
    if cross:
        trace, packed, high, low = refs
    else:
        packed, source, source_t, high, low = refs
    step, depth = buffer.shape[2], green.shape[3]
    each = depth // step
    count = high.shape[0] // step
    me = lax.axis_index("col")

    def copy(i):
        owner = lax.rem(me + 1 + i // each, n) if cross else me
        first = pl.multiple_of(owner * depth + (i % each) * step, step)
        slot = i % BUFFERS
        return pltpu.make_async_copy(green.at[0, :, pl.ds(first, step), :], buffer.at[slot], sem.at[slot])

    def store(i):
        for half in range(2):
            at = (pl.ds(i * step, step), pl.ds(half * depth, depth))
            high[at], low[at] = halves(buffer[i % BUFFERS, half])

    def multiply(i):
        result = product(high, low, packed, pl.ds(i * step, step))
        inside = pl.ds((i % each) * step, step)
        outs[i // each][inside, :] = result if cross else result + source_t[inside, :]

    for i in range(min(BUFFERS - 1, count)):
        copy(i).start()
    if not cross:
        source_t[...] = source[0].reshape(-1, depth).T

    def walk(multiplies):
        for i in range(count):
            copy(i).wait()
            if i + BUFFERS - 1 < count:
                copy(i + BUFFERS - 1).start()
            store(i)
            if multiplies and i > 0:
                multiply(i - 1)
        if multiplies:
            multiply(count - 1)

    @pl.when(active(parity))
    def _():
        if cross:
            fill(packed, [trace], True)
        walk(True)

    @pl.when(jnp.logical_not(active(parity)))
    def _():
        walk(False)


def product_kernel(parity, part, raw, high, low, *refs):
    refs = list(refs)
    if part == "own":
        outs, source_t = [refs.pop()], refs.pop(0)
    else:
        count = high.shape[0] // (high.shape[1] // 2)
        refs, outs = refs[:-count], refs[-count:]
    packed = refs.pop()

    def work():
        if refs:
            fill(packed, refs, raw)
        depth = packed.shape[0] // 2
        if part == "own":
            outs[0][...] = product(high, low, packed, pl.ds(0, depth)) + source_t[...]
        else:
            for k, out in enumerate(outs):
                out[...] = product(high, low, packed, pl.ds(k * depth, depth))

    if parity is None:
        work()
    else:
        pl.when(active(parity))(work)


def finish_kernel(*refs):
    *ins, out = refs
    value = ins[0][...]
    for ref in ins[1:]:
        value = value + ref[...]
    out[0] = value.T.reshape(out.shape[1:])


def high_rows(part, n):
    return n - 1 if part == "cross" else 1


def send(value, parity, slabs_on, cols_on):
    slabs, n = lax.axis_size("slab"), lax.axis_size("col")
    route = [
        (s * n + c, (s + slabs_on) * n + (c + cols_on) % n)
        for s in range(parity, slabs - slabs_on, 2)
        for c in range(n)
    ]
    return lax.ppermute(value, ("slab", "col"), route)


def shards(green_blocks, traces, sources):
    n = lax.axis_size("col")
    _, _, shots, depth = traces.shape
    lanes = 2 * shots
    trace = ((depth, lanes), f32)
    packing = ((2 * depth, 2 * lanes), bf16)
    rows = min(ROWS, depth)
    copying = [pltpu.VMEM((BUFFERS, 2, rows, depth), f32), pltpu.SemaphoreType.DMA((BUFFERS,))]

    def leave(step, chain, part, results):
        by = range(1, n) if part == "cross" else (0,)
        return [send(value, (chain + step) % 2, 1, k) for k, value in zip(by, results)]

    starts = {chain: send(traces, 1 - chain, 1, 0) for chain in (1, 0)}
    green, packs, after, source_t = {}, {}, (), None
    incoming = {(chain, part): [] for chain in (0, 1) for part in ("cross", "own")}
    incoming[0, "own"], incoming[1, "own"] = [starts[0]], [starts[1]]
    for step in range(STEPS):
        last = step == STEPS - 1
        arriving = {}
        for act, chain, part in ORDER[step]:
            if act == "hand":
                incoming[chain, part] = [
                    call(pass_kernel, (value,), [trace], after=after, input_output_aliases={0: 0})[0]
                    for value in incoming[chain, part]
                ]
                after = tuple(incoming[chain, part][-1:])
                continue
            cross = part == "cross"
            outs = [trace] * (n - 1 if cross else 1)
            if act == "open":
                given = [starts[chain]] if cross else [packs[chain], sources]
                first, high, low, *results = call(
                    functools.partial(opening_kernel, chain, part, n),
                    given,
                    [packing if cross else trace] + [((high_rows(part, n) * depth, 2 * depth), bf16)] * 2 + outs,
                    copying,
                    far=(green_blocks,),
                    after=after,
                )
                green[part] = [high, low]
                packs[chain], source_t = (first, source_t) if cross else (packs[chain], first)
            else:
                given = green[part] + ([] if cross else [source_t])
                given += incoming[chain, "cross"] + incoming[chain, "own"] if cross else [packs[chain]]
                results = call(
                    functools.partial(product_kernel, (chain + step) % 2, part, step == 0),
                    given,
                    [packing] + outs if cross else outs,
                    after=after,
                )
                if cross:
                    packs[chain], *results = results
            after = (results[-1],)
            arriving[chain, part] = leave(step, chain, part, results)
        if not last:
            incoming = arriving
    given = [value for key in ((1, "cross"), (1, "own"), (0, "cross"), (0, "own")) for value in incoming[key]]
    packed, *results = call(
        functools.partial(product_kernel, None, "cross", False),
        green["cross"] + given,
        [packing] + [trace] * (n - 1),
        after=after,
    )
    routes = [[(c, (c + k) % n) for c in range(n)] for k in range(1, n)]
    arrived = [lax.ppermute(value, "col", route) for value, route in zip(results, routes)]
    own = call(functools.partial(product_kernel, None, "own", False), green["own"] + [source_t, packed], [trace])
    return pl.pallas_call(
        finish_kernel,
        in_specs=[in_vmem()] * n,
        out_specs=in_vmem(),
        out_shape=jax.ShapeDtypeStruct(sources.shape, f32),
        compiler_params=pltpu.CompilerParams(vmem_limit_bytes=VMEM_LIMIT),
    )(*[pinned(a) for a in list(own) + arrived])


def solution(mesh):
    placed = P("slab", None, None, "col")
    return jax.shard_map(shards, mesh=mesh, in_specs=(placed,) * 3, out_specs=placed, check_vma=False)
```

```python
import functools

import jax
import jax.numpy as jnp
from jax import lax
from jax.experimental import pallas as pl
from jax.experimental.pallas import tpu as pltpu
from jax.sharding import PartitionSpec as P

STEPS = 4
ROWS = 128
GROUP = 2
PIECES = 2
LAG = 0
ORDER = (
    (("open", 1, "cross"), ("open", 1, "own"), ("make", 0, "cross"), ("make", 0, "own"),),
    (("hand", 1, "cross"), ("make", 1, "cross"), ("hand", 0, "cross"), ("make", 0, "cross"), ("make", 1, "own"), ("make", 0, "own"),),
    (("hand", 1, "cross"), ("hand", 0, "cross"), ("make", 1, "cross"), ("make", 1, "own"), ("make", 0, "cross"), ("make", 0, "own"),),
    (("hand", 1, "cross"), ("hand", 1, "own"), ("hand", 0, "cross"), ("hand", 0, "own"),),
)
VMEM_LIMIT = 24 << 20

f32 = jnp.float32
bf16 = jnp.bfloat16


def in_vmem():
    return pl.BlockSpec(memory_space=pltpu.VMEM)


def pinned(array):
    return pltpu.with_memory_space_constraint(array, pltpu.VMEM)


def call(kernel, args, outs, scratch=(), far=(), after=(), cost=0, **more):
    held = [pltpu.with_memory_space_constraint(a, pltpu.HBM) for a in far] + [pinned(a) for a in args]
    specs = [pl.BlockSpec(memory_space=pltpu.HBM)] * len(far) + [in_vmem()] * len(args)
    first, skip = len(held), len(after)

    def body(*refs):
        kernel(*refs[:first], *refs[first + skip :])

    return pl.pallas_call(
        body,
        in_specs=specs + [pl.BlockSpec(memory_space=pl.ANY)] * skip,
        out_specs=[in_vmem()] * len(outs),
        out_shape=[pltpu.VMEM(shape, dtype) for shape, dtype in outs],
        scratch_shapes=list(scratch),
        compiler_params=pltpu.CompilerParams(vmem_limit_bytes=VMEM_LIMIT),
        cost_estimate=pl.CostEstimate(flops=cost, bytes_accessed=0, transcendentals=0),
        **more,
    )(*held, *after)


def halves(value):
    high = value.astype(bf16)
    return high, (value - high.astype(f32)).astype(bf16)


def pass_kernel(value, out):
    pass


def product(high, low, packed, rows):
    lanes = packed.shape[1] // 2
    both = jnp.dot(high[rows, :], packed[...], preferred_element_type=f32)
    rest = jnp.dot(low[rows, :], packed[:, :lanes], preferred_element_type=f32)
    return both[:, :lanes] + both[:, lanes:] + rest


def active(parity):
    return lax.rem(lax.axis_index("slab"), 2) == parity


def fill(packed, incoming, raw):
    depth, lanes = packed.shape[0] // 2, packed.shape[1] // 2
    if raw:
        value = incoming[0][0].reshape(lanes, depth).T
    else:
        value = incoming[0][...]
        for ref in incoming[1:]:
            value = value + ref[...]
    turned = pltpu.roll(value, lanes // 2, 1)
    lane = lax.broadcasted_iota(jnp.int32, value.shape, 1)
    turned = jnp.where(lane < lanes // 2, -turned, turned)
    packed[:depth, :lanes], packed[:depth, lanes:] = halves(value)
    packed[depth:, :lanes], packed[depth:, lanes:] = halves(turned)


def opening_kernel(parity, part, n, green, *refs):
    cross = part == "cross"
    outs = n - 1 if cross else 1
    buffer, sem = refs[-2:]
    refs, outs = refs[: -2 - outs], refs[-2 - outs : -2]
    if cross:
        trace, packed, high, low = refs
    else:
        packed, source, source_t, high, low = refs
    step, depth = buffer.shape[2], green.shape[3]
    each = depth // step
    count = high.shape[0] // step
    me = lax.axis_index("col")

    def copy(i):
        owner = lax.rem(me + 1 + i // each, n) if cross else me
        first = pl.multiple_of(owner * depth + (i % each) * step, step)
        return pltpu.make_async_copy(green.at[0, :, pl.ds(first, step), :], buffer.at[i], sem.at[i])

    def store(i):
        for half in range(2):
            at = (pl.ds(i * step, step), pl.ds(half * depth, depth))
            high[at], low[at] = halves(buffer[i, half])

    def multiply(i):
        result = product(high, low, packed, pl.ds(i * step, GROUP * step))
        inside = pl.ds((i % each) * step, GROUP * step)
        outs[i // each][inside, :] = result if cross else result + source_t[inside, :]

    for i in range(count):
        copy(i).start()
    if not cross:
        source_t[...] = source[0].reshape(-1, depth).T

    def walk(multiplies):
        for i in range(count):
            copy(i).wait()
            store(i)
            if multiplies and (i + 1) % GROUP == 0 and i + 1 >= GROUP + LAG:
                multiply(i + 1 - GROUP - LAG)
        if multiplies:
            for i in range(count - LAG, count, GROUP):
                multiply(i)

    @pl.when(active(parity))
    def _():
        if cross:
            fill(packed, [trace], True)
        walk(True)

    @pl.when(jnp.logical_not(active(parity)))
    def _():
        walk(False)


def product_kernel(parity, part, raw, piece, high, low, *refs):
    refs = list(refs)
    if part == "own":
        outs, source_t = [refs.pop()], refs.pop(0)
    else:
        count = high.shape[0] // (high.shape[1] // 2)
        refs, outs = refs[:-count], refs[-count:]
    packed = refs.pop()

    def work():
        if refs and not piece:
            fill(packed, refs, raw)
        depth = packed.shape[0] // 2
        if part == "own":
            outs[0][...] = product(high, low, packed, pl.ds(0, depth)) + source_t[...]
        else:
            for k, out in enumerate(outs):
                rows = out.shape[0]
                out[...] = product(high, low, packed, pl.ds(k * depth + (piece or 0) * rows, rows))

    if parity is None:
        work()
    else:
        pl.when(active(parity))(work)


def finish_kernel(piece, aliased, *refs):
    *ins, out = refs
    if aliased:
        ins = ins[:-1]
    rows = ins[1].shape[0]
    value = ins[0][pl.ds(piece * rows, rows), :]
    for ref in ins[1:]:
        value = value + ref[...]
    out[0] = value.T.reshape(out.shape[1:])


def high_rows(part, n):
    return n - 1 if part == "cross" else 1


def send(value, parity, slabs_on, cols_on):
    slabs, n = lax.axis_size("slab"), lax.axis_size("col")
    route = [
        (s * n + c, (s + slabs_on) * n + (c + cols_on) % n)
        for s in range(parity, slabs - slabs_on, 2)
        for c in range(n)
    ]
    return lax.ppermute(value, ("slab", "col"), route)


def shards(green_blocks, traces, sources):
    n = lax.axis_size("col")
    _, _, shots, depth = traces.shape
    lanes = 2 * shots
    trace = ((depth, lanes), f32)
    packing = ((2 * depth, 2 * lanes), bf16)
    rows = min(ROWS, depth // GROUP)

    def copying(part):
        count = high_rows(part, n) * depth // rows
        return [pltpu.VMEM((count, 2, rows, depth), f32), pltpu.SemaphoreType.DMA((count,))]

    def leave(step, chain, part, results):
        by = range(1, n) if part == "cross" else (0,)
        return [send(value, (chain + step) % 2, 1, k) for k, value in zip(by, results)]

    starts = {chain: send(traces, 1 - chain, 1, 0) for chain in (1, 0)}
    green, packs, after, source_t = {}, {}, (), None
    incoming = {(chain, part): [] for chain in (0, 1) for part in ("cross", "own")}
    incoming[0, "own"], incoming[1, "own"] = [starts[0]], [starts[1]]
    for step in range(STEPS):
        last = step == STEPS - 1
        arriving = {}
        for act, chain, part in ORDER[step]:
            if act == "hand":
                incoming[chain, part] = [
                    call(pass_kernel, (value,), [trace], after=after, input_output_aliases={0: 0})[0]
                    for value in incoming[chain, part]
                ]
                after = tuple(incoming[chain, part][-1:])
                continue
            cross = part == "cross"
            outs = [trace] * (n - 1 if cross else 1)
            if act == "open":
                given = [starts[chain]] if cross else [packs[chain], sources]
                first, high, low, *results = call(
                    functools.partial(opening_kernel, chain, part, n),
                    given,
                    [packing if cross else trace] + [((high_rows(part, n) * depth, 2 * depth), bf16)] * 2 + outs,
                    copying(part),
                    far=(green_blocks,),
                    after=after,
                )
                green[part] = [high, low]
                packs[chain], source_t = (first, source_t) if cross else (packs[chain], first)
            else:
                given = green[part] + ([] if cross else [source_t])
                given += incoming[chain, "cross"] + incoming[chain, "own"] if cross else [packs[chain]]
                results = call(
                    functools.partial(product_kernel, (chain + step) % 2, part, step == 0, None),
                    given,
                    [packing] + outs if cross else outs,
                    after=after,
                )
                if cross:
                    packs[chain], *results = results
            after = (results[-1],)
            arriving[chain, part] = leave(step, chain, part, results)
        if not last:
            incoming = arriving
    given = [value for key in ((1, "cross"), (1, "own"), (0, "cross"), (0, "own")) for value in incoming[key]]
    routes = [[(c, (c + k) % n) for c in range(n)] for k in range(1, n)]
    piece = depth // PIECES
    arrived = []
    for i in range(PIECES):
        packed, *results = call(
            functools.partial(product_kernel, None, "cross", False, i),
            green["cross"] + given,
            [packing] + [((piece, lanes), f32)] * (n - 1),
            after=after,
        ) if i == 0 else (packed,) + tuple(call(
            functools.partial(product_kernel, None, "cross", False, i),
            green["cross"] + [packed],
            [((piece, lanes), f32)] * (n - 1),
            after=after,
        ))
        after = (results[-1],)
        arrived.append([lax.ppermute(value, "col", route) for value, route in zip(results, routes)])
    (own,) = call(
        functools.partial(product_kernel, None, "own", False, None), green["own"] + [source_t, packed], [trace], after=after
    )
    out = None
    for i in range(PIECES):
        ins = [own] + arrived[i]
        out = pl.pallas_call(
            functools.partial(finish_kernel, i, out is not None),
            grid=(1,),
            in_specs=[pl.BlockSpec(memory_space=pltpu.VMEM)] * n + [pl.BlockSpec(memory_space=pl.ANY)] * (out is not None),
            out_specs=pl.BlockSpec((1, 2, shots, piece), functools.partial(lambda i, _: (0, 0, 0, i), i)),
            out_shape=jax.ShapeDtypeStruct(sources.shape, f32),
            input_output_aliases={} if out is None else {n: 0},
            compiler_params=pltpu.CompilerParams(vmem_limit_bytes=VMEM_LIMIT),
        )(*[pinned(a) for a in ins], *([] if out is None else [out]))
    return out


def solution(mesh):
    placed = P("slab", None, None, "col")
    return jax.shard_map(shards, mesh=mesh, in_specs=(placed,) * 3, out_specs=placed, check_vma=False)
```

```python
import functools

import jax
import jax.numpy as jnp
from jax import lax
from jax.experimental import pallas as pl
from jax.experimental.pallas import tpu as pltpu
from jax.sharding import PartitionSpec as P

STEPS = 4
ROWS = 128
GROUP = 2
PIECES = 4
LANES = 128
LAG = 0
ORDER = (
    (("open", 1, "cross"), ("open", 1, "own"), ("make", 0, "cross"), ("make", 0, "own"),),
    (("hand", 1, "cross"), ("make", 1, "cross"), ("hand", 0, "cross"), ("make", 0, "own"), ("make", 1, "own"), ("make", 0, "cross"),),
    (("hand", 1, "cross"), ("hand", 0, "own"), ("hand", 1, "own"), ("make", 1, "cross"), ("make", 1, "own"), ("hand", 0, "cross"), ("make", 0, "cross"), ("make", 0, "own"),),
    (("hand", 1, "cross"), ("hand", 1, "own"), ("hand", 0, "cross"), ("hand", 0, "own"),),
)
VMEM_LIMIT = 24 << 20

f32 = jnp.float32
bf16 = jnp.bfloat16


def in_vmem():
    return pl.BlockSpec(memory_space=pltpu.VMEM)


def pinned(array):
    return pltpu.with_memory_space_constraint(array, pltpu.VMEM)


def call(kernel, args, outs, scratch=(), far=(), after=(), cost=0, **more):
    held = [pltpu.with_memory_space_constraint(a, pltpu.HBM) for a in far] + [pinned(a) for a in args]
    specs = [pl.BlockSpec(memory_space=pltpu.HBM)] * len(far) + [in_vmem()] * len(args)
    first, skip = len(held), len(after)

    def body(*refs):
        kernel(*refs[:first], *refs[first + skip :])

    return pl.pallas_call(
        body,
        in_specs=specs + [pl.BlockSpec(memory_space=pl.ANY)] * skip,
        out_specs=[in_vmem()] * len(outs),
        out_shape=[pltpu.VMEM(shape, dtype) for shape, dtype in outs],
        scratch_shapes=list(scratch),
        compiler_params=pltpu.CompilerParams(vmem_limit_bytes=VMEM_LIMIT),
        cost_estimate=pl.CostEstimate(flops=cost, bytes_accessed=0, transcendentals=0),
        **more,
    )(*held, *after)


def halves(value):
    high = value.astype(bf16)
    return high, (value - high.astype(f32)).astype(bf16)


def pass_kernel(value, out):
    pass


def product(high, low, packed, rows):
    lanes = packed.shape[1] // 2
    both = jnp.dot(high[rows, :], packed[...], preferred_element_type=f32)
    rest = jnp.dot(low[rows, :], packed[:, :lanes], preferred_element_type=f32)
    return both[:, :lanes] + both[:, lanes:] + rest


def active(parity):
    return lax.rem(lax.axis_index("slab"), 2) == parity


def fill(packed, incoming, raw):
    depth, lanes = packed.shape[0] // 2, packed.shape[1] // 2
    if raw:
        value = incoming[0][0].reshape(lanes, depth).T
    else:
        value = incoming[0][...]
        for ref in incoming[1:]:
            value = value + ref[...]
    turned = pltpu.roll(value, lanes // 2, 1)
    lane = lax.broadcasted_iota(jnp.int32, value.shape, 1)
    turned = jnp.where(lane < lanes // 2, -turned, turned)
    packed[:depth, :lanes], packed[:depth, lanes:] = halves(value)
    packed[depth:, :lanes], packed[depth:, lanes:] = halves(turned)


def opening_kernel(parity, part, n, green, *refs):
    buffer, sem = refs[-2:]
    if part == "cross":
        trace, packed, high, low, *outs = refs[:-2]
    else:
        packed, source, _, _, source_t, high, low, high_cross, low_cross, *outs = refs[:-2]
    step, depth = buffer.shape[2], green.shape[3]
    each = depth // step
    me = lax.axis_index("col")

    def walk(chunks, multiplies):
        def copy(i):
            owner, place = chunks[i][:2]
            first = pl.multiple_of(owner * depth + place * step, step)
            return pltpu.make_async_copy(green.at[0, :, pl.ds(first, step), :], buffer.at[i], sem.at[i])

        for i in range(len(chunks)):
            copy(i).start()
        if multiplies and part == "cross":
            fill(packed, [trace], True)
        if part == "own":
            source_t[...] = source[0].reshape(-1, depth).T
        lanes = packed.shape[1] // 2
        for j in range(0, len(chunks), GROUP):
            both, rest = None, None
            for i in range(j, j + GROUP):
                copy(i).wait()
            _, place, (high_to, low_to), to = chunks[j]
            for half in range(2):
                at = (pl.ds(to * step, GROUP * step), pl.ds(half * depth, depth))
                upper, lower = halves(jnp.concatenate([buffer[i, half] for i in range(j, j + GROUP)], 0))
                high_to[at], low_to[at] = upper, lower
                if multiplies:
                    weights = packed[pl.ds(half * depth, depth), :]
                    one = jnp.dot(upper, weights, preferred_element_type=f32)
                    two = jnp.dot(lower, weights[:, :lanes], preferred_element_type=f32)
                    both, rest = (one, two) if half == 0 else (both + one, rest + two)
            if multiplies:
                result = both[:, :lanes] + both[:, lanes:] + rest
                inside = pl.ds(place * step, GROUP * step)
                outs[to // each][inside, :] = result if part == "cross" else result + source_t[inside, :]

    def chunks_of(part, to):
        if part == "own":
            return [(me, i, to, i) for i in range(each)]
        return [(lax.rem(me + 1 + k, n), i, to, k * each + i) for k in range(n - 1) for i in range(each)]

    @pl.when(active(parity))
    def _():
        walk(chunks_of(part, (high, low)), True)

    if part == "own":

        @pl.when(jnp.logical_not(active(parity)))
        def _():
            walk(chunks_of("cross", (high_cross, low_cross)) + chunks_of("own", (high, low)), False)


def product_kernel(parity, part, raw, piece, high, low, *refs):
    refs = list(refs)
    if part == "own":
        outs, source_t = [refs.pop()], refs.pop(0)
    else:
        count = high.shape[0] // (high.shape[1] // 2)
        refs, outs = refs[:-count], refs[-count:]
    packed = refs.pop()

    def work():
        if refs and not piece:
            fill(packed, refs, raw)
        depth = packed.shape[0] // 2
        if part == "own":
            outs[0][...] = product(high, low, packed, pl.ds(0, depth)) + source_t[...]
        else:
            for k, out in enumerate(outs):
                rows = out.shape[0]
                out[...] = product(high, low, packed, pl.ds(k * depth + (piece or 0) * rows, rows))

    if parity is None:
        work()
    else:
        pl.when(active(parity))(work)


def finish_kernel(piece, aliased, *refs):
    *ins, out = refs
    if aliased:
        ins = ins[:-1]
    rows = ins[1].shape[0]
    value = ins[0][pl.ds(piece * rows, rows), :]
    for ref in ins[1:]:
        value = value + ref[...]
    out[0] = value.T.reshape(out.shape[1:])


def high_rows(part, n):
    return n - 1 if part == "cross" else 1


def send(value, parity, slabs_on, cols_on):
    slabs, n = lax.axis_size("slab"), lax.axis_size("col")
    route = [
        (s * n + c, (s + slabs_on) * n + (c + cols_on) % n)
        for s in range(parity, slabs - slabs_on, 2)
        for c in range(n)
    ]
    return lax.ppermute(value, ("slab", "col"), route)


def shards(green_blocks, traces, sources):
    n = lax.axis_size("col")
    _, _, shots, depth = traces.shape
    lanes = 2 * shots
    trace = ((depth, lanes), f32)
    packing = ((2 * depth, 2 * lanes), bf16)
    rows = min(ROWS, depth // GROUP)

    def copying(part):
        count = (n - 1 if part == "cross" else n) * depth // rows
        return [pltpu.VMEM((count, 2, rows, depth), f32), pltpu.SemaphoreType.DMA((count,))]

    def leave(step, chain, part, results):
        by = range(1, n) if part == "cross" else (0,)
        return [send(value, (chain + step) % 2, 1, k) for k, value in zip(by, results)]

    starts = {chain: send(traces, 1 - chain, 1, 0) for chain in (1, 0)}
    green, packs, after, source_t = {}, {}, (), None
    incoming = {(chain, part): [] for chain in (0, 1) for part in ("cross", "own")}
    incoming[0, "own"], incoming[1, "own"] = [starts[0]], [starts[1]]
    for step in range(STEPS):
        last = step == STEPS - 1
        arriving = {}
        for act, chain, part in ORDER[step]:
            if act == "hand":
                incoming[chain, part] = [
                    call(pass_kernel, (value,), [trace], after=after, input_output_aliases={0: 0})[0]
                    for value in incoming[chain, part]
                ]
                after = tuple(incoming[chain, part][-1:])
                continue
            cross = part == "cross"
            outs = [trace] * (n - 1 if cross else 1)
            opening = not any(key[0] == chain for key in arriving)
            if act == "open":
                given = [starts[chain]] if cross else [packs[chain], sources, *green["cross"]]
                sized = [((high_rows(kind, n) * depth, 2 * depth), bf16) for kind in ("cross", "own") for _ in range(2)]
                first, high, low, *results = call(
                    functools.partial(opening_kernel, chain, part, n),
                    given,
                    [packing] + sized[:2] + outs if cross else [trace] + sized[2:] + sized[:2] + outs,
                    copying(part),
                    far=(green_blocks,),
                    after=after,
                    input_output_aliases={} if cross else {3: 3, 4: 4},
                )
                green[part] = [high, low]
                if cross:
                    packs[chain] = first
                else:
                    source_t = first
                    green["cross"], results = results[:2], results[2:]
            else:
                given = green[part] + ([] if cross else [source_t])
                given += incoming[chain, "cross"] + incoming[chain, "own"] if opening else [packs[chain]]
                results = call(
                    functools.partial(product_kernel, (chain + step) % 2, part, step == 0, None),
                    given,
                    [packing] + outs if opening else outs,
                    after=after,
                )
                if opening:
                    packs[chain], *results = results
            after = (results[-1],)
            arriving[chain, part] = leave(step, chain, part, results)
        if not last:
            incoming = arriving
    given = [value for key in ((1, "cross"), (1, "own"), (0, "cross"), (0, "own")) for value in incoming[key]]
    routes = [[(c, (c + k) % n) for c in range(n)] for k in range(1, n)]
    pieces = max(1, min(PIECES, depth // LANES))
    piece = depth // pieces
    arrived = []
    for i in range(pieces):
        packed, *results = call(
            functools.partial(product_kernel, None, "cross", False, i),
            green["cross"] + given,
            [packing] + [((piece, lanes), f32)] * (n - 1),
            after=after,
        ) if i == 0 else (packed,) + tuple(call(
            functools.partial(product_kernel, None, "cross", False, i),
            green["cross"] + [packed],
            [((piece, lanes), f32)] * (n - 1),
            after=after,
        ))
        after = (results[-1],)
        arrived.append([lax.ppermute(value, "col", route) for value, route in zip(results, routes)])
    (own,) = call(
        functools.partial(product_kernel, None, "own", False, None), green["own"] + [source_t, packed], [trace], after=after
    )
    out = None
    for i in range(pieces):
        ins = [own] + arrived[i]
        out = pl.pallas_call(
            functools.partial(finish_kernel, i, out is not None),
            grid=(1,),
            in_specs=[pl.BlockSpec(memory_space=pltpu.VMEM)] * n + [pl.BlockSpec(memory_space=pl.ANY)] * (out is not None),
            out_specs=pl.BlockSpec((1, 2, shots, piece), functools.partial(lambda i, _: (0, 0, 0, i), i)),
            out_shape=jax.ShapeDtypeStruct(sources.shape, f32),
            input_output_aliases={} if out is None else {n: 0},
            compiler_params=pltpu.CompilerParams(vmem_limit_bytes=VMEM_LIMIT),
        )(*[pinned(a) for a in ins], *([] if out is None else [out]))
    return out


def solution(mesh):
    placed = P("slab", None, None, "col")
    return jax.shard_map(shards, mesh=mesh, in_specs=(placed,) * 3, out_specs=placed, check_vma=False)
```

```python
import functools

import jax
import jax.numpy as jnp
from jax import lax
from jax.experimental import pallas as pl
from jax.experimental.pallas import tpu as pltpu
from jax.sharding import PartitionSpec as P

STEPS = 4
ROWS = 128
GROUP = 2
AHEAD = 4
PIECES = 4
LANES = 128
LAG = 0
ORDER = (
    (("open", 1, "cross"), ("open", 1, "own"), ("make", 0, "cross"), ("make", 0, "own"),),
    (("hand", 1, "cross"), ("make", 1, "cross"), ("hand", 0, "cross"), ("make", 0, "own"), ("make", 1, "own"), ("make", 0, "cross"),),
    (("hand", 1, "cross"), ("hand", 0, "own"), ("hand", 1, "own"), ("make", 1, "cross"), ("make", 1, "own"), ("hand", 0, "cross"), ("make", 0, "cross"), ("make", 0, "own"),),
    (("hand", 1, "cross"), ("hand", 1, "own"), ("hand", 0, "cross"), ("hand", 0, "own"),),
)
VMEM_LIMIT = 24 << 20

f32 = jnp.float32
bf16 = jnp.bfloat16


def in_vmem():
    return pl.BlockSpec(memory_space=pltpu.VMEM)


def pinned(array):
    return pltpu.with_memory_space_constraint(array, pltpu.VMEM)


def call(kernel, args, outs, scratch=(), far=(), after=(), cost=0, **more):
    held = [pltpu.with_memory_space_constraint(a, pltpu.HBM) for a in far] + [pinned(a) for a in args]
    specs = [pl.BlockSpec(memory_space=pltpu.HBM)] * len(far) + [in_vmem()] * len(args)
    first, skip = len(held), len(after)

    def body(*refs):
        kernel(*refs[:first], *refs[first + skip :])

    return pl.pallas_call(
        body,
        in_specs=specs + [pl.BlockSpec(memory_space=pl.ANY)] * skip,
        out_specs=[in_vmem()] * len(outs),
        out_shape=[pltpu.VMEM(shape, dtype) for shape, dtype in outs],
        scratch_shapes=list(scratch),
        compiler_params=pltpu.CompilerParams(vmem_limit_bytes=VMEM_LIMIT),
        cost_estimate=pl.CostEstimate(flops=cost, bytes_accessed=0, transcendentals=0),
        **more,
    )(*held, *after)


def halves(value):
    high = value.astype(bf16)
    return high, (value - high.astype(f32)).astype(bf16)


def hold_kernel(value, out):
    out[...] = jnp.zeros_like(out)


def product(high, low, packed, rows):
    lanes = packed.shape[1] // 2
    both = jnp.dot(high[rows, :], packed[...], preferred_element_type=f32)
    rest = jnp.dot(low[rows, :], packed[:, :lanes], preferred_element_type=f32)
    return both[:, :lanes] + both[:, lanes:] + rest


def active(parity):
    return lax.rem(lax.axis_index("slab"), 2) == parity


def fill(packed, incoming, raw):
    depth, lanes = packed.shape[0] // 2, packed.shape[1] // 2
    if raw:
        value = incoming[0][0].reshape(lanes, depth).T
    else:
        value = incoming[0][...]
        for ref in incoming[1:]:
            value = value + ref[...]
    turned = pltpu.roll(value, lanes // 2, 1)
    lane = lax.broadcasted_iota(jnp.int32, value.shape, 1)
    turned = jnp.where(lane < lanes // 2, -turned, turned)
    packed[:depth, :lanes], packed[:depth, lanes:] = halves(value)
    packed[depth:, :lanes], packed[depth:, lanes:] = halves(turned)


def opening_kernel(parity, part, n, green, *refs):
    buffer, sem = refs[-2:]
    if part == "cross":
        trace, packed, ahead, high, low, *outs = refs[:-2]
    else:
        packed, ahead, source, source_t, high, low, high_cross, low_cross, *outs = refs[:-2]
    step, depth = buffer.shape[2], green.shape[3]
    each = depth // step
    me = lax.axis_index("col")

    def walk(chunks, multiplies, early=0, then=lambda: None):
        def copy(i):
            owner, place = chunks[i][:2]
            first = pl.multiple_of(owner * depth + place * step, step)
            return pltpu.make_async_copy(green.at[0, :, pl.ds(first, step), :], buffer.at[i], sem.at[i])

        def rows(i, half):
            return ahead[half, pl.ds(i * step, step), :] if i < early else buffer[i, half]

        for i in range(early, len(chunks)):
            copy(i).start()
        then()
        if multiplies and part == "cross":
            fill(packed, [trace], True)
        if part == "own":
            source_t[...] = source[0].reshape(-1, depth).T
        lanes = packed.shape[1] // 2
        for j in range(0, len(chunks), GROUP):
            both, rest = None, None
            for i in range(max(j, early), j + GROUP):
                copy(i).wait()
            _, place, (high_to, low_to), to = chunks[j]
            for half in range(2):
                at = (pl.ds(to * step, GROUP * step), pl.ds(half * depth, depth))
                upper, lower = halves(jnp.concatenate([rows(i, half) for i in range(j, j + GROUP)], 0))
                high_to[at], low_to[at] = upper, lower
                if multiplies:
                    weights = packed[pl.ds(half * depth, depth), :]
                    one = jnp.dot(upper, weights, preferred_element_type=f32)
                    two = jnp.dot(lower, weights[:, :lanes], preferred_element_type=f32)
                    both, rest = (one, two) if half == 0 else (both + one, rest + two)
            if multiplies:
                result = both[:, :lanes] + both[:, lanes:] + rest
                inside = pl.ds(place * step, GROUP * step)
                outs[to // each][inside, :] = result if part == "cross" else result + source_t[inside, :]

    def chunks_of(part, to):
        if part == "own":
            return [(me, i, to, i) for i in range(each)]
        return [(lax.rem(me + 1 + k, n), i, to, k * each + i) for k in range(n - 1) for i in range(each)]

    held = ahead.shape[1] // step

    def ahead_copy(i):
        first = pl.multiple_of(me * depth + i * step, step)
        place = ahead.at[:, pl.ds(i * step, step), :]
        return pltpu.make_async_copy(green.at[0, :, pl.ds(first, step), :], place, sem.at[(n - 1) * each + i])

    @pl.when(active(parity))
    def _():
        if part == "cross":
            walk(chunks_of(part, (high, low)), True, then=lambda: [ahead_copy(i).start() for i in range(held)])
            for i in range(held):
                ahead_copy(i).wait()
        else:
            walk(chunks_of(part, (high, low)), True, held)

    if part == "own":

        @pl.when(jnp.logical_not(active(parity)))
        def _():
            walk(chunks_of("cross", (high_cross, low_cross)) + chunks_of("own", (high, low)), False)


def product_kernel(parity, part, raw, piece, high, low, *refs):
    refs = list(refs)
    if part == "own":
        outs, source_t = [refs.pop()], refs.pop(0)
    else:
        count = high.shape[0] // (high.shape[1] // 2)
        refs, outs = refs[:-count], refs[-count:]
    packed = refs.pop()

    def work():
        if refs and not piece:
            fill(packed, refs, raw)
        depth = packed.shape[0] // 2
        if part == "own":
            outs[0][...] = product(high, low, packed, pl.ds(0, depth)) + source_t[...]
        else:
            for k, out in enumerate(outs):
                rows = out.shape[0]
                out[...] = product(high, low, packed, pl.ds(k * depth + (piece or 0) * rows, rows))

    if parity is None:
        work()
    else:
        pl.when(active(parity))(work)


def last_cross_kernel(piece, high_even, low_even, high_odd, low_odd, *refs):
    for parity, high, low in ((0, high_even, low_even), (1, high_odd, low_odd)):
        product_kernel(parity, "cross", False, piece, high, low, *refs)


def finish_kernel(piece, aliased, *refs):
    *ins, out = refs
    if aliased:
        ins = ins[:-1]
    rows = ins[1].shape[0]
    value = ins[0][pl.ds(piece * rows, rows), :]
    for ref in ins[1:]:
        value = value + ref[...]
    out[0] = value.T.reshape(out.shape[1:])


def high_rows(part, n):
    return n - 1 if part == "cross" else 1


def send(value, parity, slabs_on, cols_on):
    slabs, n = lax.axis_size("slab"), lax.axis_size("col")
    route = [
        (s * n + c, (s + slabs_on) * n + (c + cols_on) % n)
        for s in range(parity, slabs - slabs_on, 2)
        for c in range(n)
    ]
    return lax.ppermute(value, ("slab", "col"), route)


def shards(green_blocks, traces, sources):
    n = lax.axis_size("col")
    _, _, shots, depth = traces.shape
    lanes = 2 * shots
    trace = ((depth, lanes), f32)
    packing = ((2 * depth, 2 * lanes), bf16)
    rows = min(ROWS, depth // GROUP)

    def copying(part):
        count = (n - 1 if part == "cross" else n) * depth // rows
        return [pltpu.VMEM((count, 2, rows, depth), f32), pltpu.SemaphoreType.DMA((n * depth // rows,))]

    early = ((2, max(depth // AHEAD // rows, 1) * rows, depth), f32)

    def leave(step, chain, part, results):
        by = range(1, n) if part == "cross" else (0,)
        return [send(value, (chain + step) % 2, 1, k) for k, value in zip(by, results)]

    starts = {chain: send(traces, 1 - chain, 1, 0) for chain in (1, 0)}
    green, packs, after, source_t = {}, {}, (), None
    incoming = {(chain, part): [] for chain in (0, 1) for part in ("cross", "own")}
    incoming[0, "own"], incoming[1, "own"] = [starts[0]], [starts[1]]
    for step in range(STEPS):
        last = step == STEPS - 1
        arriving = {}
        for act, chain, part in ORDER[step]:
            if act == "hand":
                for value in incoming[chain, part]:
                    after = tuple(call(hold_kernel, (value,), [((8, lanes), f32)], after=after))
                continue
            cross = part == "cross"
            outs = [trace] * (n - 1 if cross else 1)
            opening = not any(key[0] == chain for key in arriving)
            if act == "open":
                given = [starts[chain]] if cross else [packs[chain], ahead, sources]
                sized = [((high_rows(kind, n) * depth, 2 * depth), bf16) for kind in ("cross", "own") for _ in range(2)]
                first, *results = call(
                    functools.partial(opening_kernel, chain, part, n),
                    given,
                    [packing, early] + sized[:2] + outs if cross else [trace] + sized[2:] + sized[:2] + outs,
                    copying(part),
                    far=(green_blocks,),
                    after=after,
                )
                if cross:
                    ahead, *results = results
                high, low, *results = results
                if cross:
                    packs[chain], green["cross", chain] = first, [high, low]
                else:
                    source_t, green["own"] = first, [high, low]
                    green["cross", 1 - chain], results = results[:2], results[2:]
            else:
                given = green["cross", (chain + step) % 2] if cross else green["own"] + [source_t]
                given = given + (incoming[chain, "cross"] + incoming[chain, "own"] if opening else [packs[chain]])
                results = call(
                    functools.partial(product_kernel, (chain + step) % 2, part, step == 0, None),
                    given,
                    [packing] + outs if opening else outs,
                    after=after,
                )
                if opening:
                    packs[chain], *results = results
            after = (results[-1],)
            arriving[chain, part] = leave(step, chain, part, results)
        if not last:
            incoming = arriving
    given = [value for key in ((1, "cross"), (1, "own"), (0, "cross"), (0, "own")) for value in incoming[key]]
    routes = [[(c, (c + k) % n) for c in range(n)] for k in range(1, n)]
    pieces = max(1, min(PIECES, depth // LANES))
    piece = depth // pieces
    arrived = []
    for i in range(pieces):
        packed, *results = call(
            functools.partial(last_cross_kernel, i),
            green["cross", 0] + green["cross", 1] + given,
            [packing] + [((piece, lanes), f32)] * (n - 1),
            after=after,
        ) if i == 0 else (packed,) + tuple(call(
            functools.partial(last_cross_kernel, i),
            green["cross", 0] + green["cross", 1] + [packed],
            [((piece, lanes), f32)] * (n - 1),
            after=after,
        ))
        after = (results[-1],)
        arrived.append([lax.ppermute(value, "col", route) for value, route in zip(results, routes)])
    (own,) = call(
        functools.partial(product_kernel, None, "own", False, None), green["own"] + [source_t, packed], [trace], after=after
    )
    out = None
    for i in range(pieces):
        ins = [own] + arrived[i]
        out = pl.pallas_call(
            functools.partial(finish_kernel, i, out is not None),
            grid=(1,),
            in_specs=[pl.BlockSpec(memory_space=pltpu.VMEM)] * n + [pl.BlockSpec(memory_space=pl.ANY)] * (out is not None),
            out_specs=pl.BlockSpec((1, 2, shots, piece), functools.partial(lambda i, _: (0, 0, 0, i), i)),
            out_shape=jax.ShapeDtypeStruct(sources.shape, f32),
            input_output_aliases={} if out is None else {n: 0},
            compiler_params=pltpu.CompilerParams(vmem_limit_bytes=VMEM_LIMIT),
        )(*[pinned(a) for a in ins], *([] if out is None else [out]))
    return out


def solution(mesh):
    placed = P("slab", None, None, "col")
    return jax.shard_map(shards, mesh=mesh, in_specs=(placed,) * 3, out_specs=placed, check_vma=False)
```

```python
import functools

import jax
import jax.numpy as jnp
from jax import lax
from jax.experimental import pallas as pl
from jax.experimental.pallas import tpu as pltpu
from jax.sharding import PartitionSpec as P

STEPS = 4
ROWS = 128
GROUP = 2
AHEAD = 8
PIECES = 4
LANES = 128
LAG = 0
ORDER = (
    (("open", 1, "cross"), ("open", 1, "own"), ("make", 0, "cross"), ("make", 0, "own"),),
    (("hand", 1, "cross"), ("make", 1, "cross"), ("hand", 0, "cross"), ("make", 0, "own"), ("make", 1, "own"), ("make", 0, "cross"),),
    (("hand", 1, "cross"), ("hand", 0, "own"), ("hand", 1, "own"), ("make", 1, "cross"), ("make", 1, "own"), ("hand", 0, "cross"), ("make", 0, "cross"), ("make", 0, "own"),),
    (("hand", 1, "cross"), ("hand", 1, "own"), ("hand", 0, "cross"), ("hand", 0, "own"),),
)
VMEM_LIMIT = 24 << 20

f32 = jnp.float32
bf16 = jnp.bfloat16


def in_vmem():
    return pl.BlockSpec(memory_space=pltpu.VMEM)


def pinned(array):
    return pltpu.with_memory_space_constraint(array, pltpu.VMEM)


def call(kernel, args, outs, scratch=(), far=(), after=(), cost=0, **more):
    held = [pltpu.with_memory_space_constraint(a, pltpu.HBM) for a in far] + [pinned(a) for a in args]
    specs = [pl.BlockSpec(memory_space=pltpu.HBM)] * len(far) + [in_vmem()] * len(args)
    first, skip = len(held), len(after)

    def body(*refs):
        kernel(*refs[:first], *refs[first + skip :])

    return pl.pallas_call(
        body,
        in_specs=specs + [pl.BlockSpec(memory_space=pl.ANY)] * skip,
        out_specs=[in_vmem()] * len(outs),
        out_shape=[pltpu.VMEM(shape, dtype) for shape, dtype in outs],
        scratch_shapes=list(scratch),
        compiler_params=pltpu.CompilerParams(vmem_limit_bytes=VMEM_LIMIT),
        cost_estimate=pl.CostEstimate(flops=cost, bytes_accessed=0, transcendentals=0),
        **more,
    )(*held, *after)


def halves(value):
    high = value.astype(bf16)
    return high, (value - high.astype(f32)).astype(bf16)


def hold_kernel(value, out):
    out[...] = jnp.zeros_like(out)


def product(high, low, packed, rows):
    lanes = packed.shape[1] // 2
    both = jnp.dot(high[rows, :], packed[...], preferred_element_type=f32)
    rest = jnp.dot(low[rows, :], packed[:, :lanes], preferred_element_type=f32)
    return both[:, :lanes] + both[:, lanes:] + rest


def active(parity):
    return lax.rem(lax.axis_index("slab"), 2) == parity


def fill(packed, incoming, raw):
    depth, lanes = packed.shape[0] // 2, packed.shape[1] // 2
    if raw:
        value = incoming[0][0].reshape(lanes, depth).T
    else:
        value = incoming[0][...]
        for ref in incoming[1:]:
            value = value + ref[...]
    turned = pltpu.roll(value, lanes // 2, 1)
    lane = lax.broadcasted_iota(jnp.int32, value.shape, 1)
    turned = jnp.where(lane < lanes // 2, -turned, turned)
    packed[:depth, :lanes], packed[:depth, lanes:] = halves(value)
    packed[depth:, :lanes], packed[depth:, lanes:] = halves(turned)


def opening_kernel(parity, part, n, green, *refs):
    buffer, sem = refs[-2:]
    if part == "cross":
        trace, packed, ahead, high, low, *outs = refs[:-2]
    else:
        packed, ahead, source, source_t, high, low, high_cross, low_cross, *outs = refs[:-2]
    step, depth = buffer.shape[2], green.shape[3]
    each = depth // step
    me = lax.axis_index("col")

    def walk(chunks, multiplies, early=0, then=lambda: None):
        def copy(i):
            owner, place = chunks[i][:2]
            first = pl.multiple_of(owner * depth + place * step, step)
            return pltpu.make_async_copy(green.at[0, :, pl.ds(first, step), :], buffer.at[i], sem.at[i])

        def rows(i, half):
            return ahead[half, pl.ds(i * step, step), :] if i < early else buffer[i, half]

        for i in range(early, len(chunks)):
            copy(i).start()
        then()
        if multiplies and part == "cross":
            fill(packed, [trace], True)
        if part == "own":
            source_t[...] = source[0].reshape(-1, depth).T
        lanes = packed.shape[1] // 2
        for j in range(0, len(chunks), GROUP):
            both, rest = None, None
            for i in range(max(j, early), j + GROUP):
                copy(i).wait()
            _, place, (high_to, low_to), to = chunks[j]
            for half in range(2):
                at = (pl.ds(to * step, GROUP * step), pl.ds(half * depth, depth))
                upper, lower = halves(jnp.concatenate([rows(i, half) for i in range(j, j + GROUP)], 0))
                high_to[at], low_to[at] = upper, lower
                if multiplies:
                    weights = packed[pl.ds(half * depth, depth), :]
                    one = jnp.dot(upper, weights, preferred_element_type=f32)
                    two = jnp.dot(lower, weights[:, :lanes], preferred_element_type=f32)
                    both, rest = (one, two) if half == 0 else (both + one, rest + two)
            if multiplies:
                result = both[:, :lanes] + both[:, lanes:] + rest
                inside = pl.ds(place * step, GROUP * step)
                outs[to // each][inside, :] = result if part == "cross" else result + source_t[inside, :]

    def chunks_of(part, to):
        if part == "own":
            return [(me, i, to, i) for i in range(each)]
        return [(lax.rem(me + 1 + k, n), i, to, k * each + i) for k in range(n - 1) for i in range(each)]

    held = ahead.shape[1] // step

    def ahead_copy(i):
        first = pl.multiple_of(me * depth + i * step, step)
        place = ahead.at[:, pl.ds(i * step, step), :]
        return pltpu.make_async_copy(green.at[0, :, pl.ds(first, step), :], place, sem.at[(n - 1) * each + i])

    @pl.when(active(parity))
    def _():
        if part == "cross":
            walk(chunks_of(part, (high, low)), True, then=lambda: [ahead_copy(i).start() for i in range(held)])
            for i in range(held):
                ahead_copy(i).wait()
        else:
            walk(chunks_of(part, (high, low)), True, held)

    if part == "own":

        @pl.when(jnp.logical_not(active(parity)))
        def _():
            walk(chunks_of("cross", (high_cross, low_cross)) + chunks_of("own", (high, low)), False)


def product_kernel(parity, part, raw, piece, high, low, *refs):
    refs = list(refs)
    if part == "own":
        outs, source_t = [refs.pop()], refs.pop(0)
    else:
        count = high.shape[0] // (high.shape[1] // 2)
        refs, outs = refs[:-count], refs[-count:]
    packed = refs.pop()

    def work():
        if refs and not piece:
            fill(packed, refs, raw)
        depth = packed.shape[0] // 2
        if part == "own":
            outs[0][...] = product(high, low, packed, pl.ds(0, depth)) + source_t[...]
        else:
            for k, out in enumerate(outs):
                rows = out.shape[0]
                out[...] = product(high, low, packed, pl.ds(k * depth + (piece or 0) * rows, rows))

    if parity is None:
        work()
    else:
        pl.when(active(parity))(work)


def last_cross_kernel(piece, high_even, low_even, high_odd, low_odd, *refs):
    for parity, high, low in ((0, high_even, low_even), (1, high_odd, low_odd)):
        product_kernel(parity, "cross", False, piece, high, low, *refs)


def finish_kernel(piece, aliased, *refs):
    *ins, out = refs
    if aliased:
        ins = ins[:-1]
    rows = ins[1].shape[0]
    value = ins[0][pl.ds(piece * rows, rows), :]
    for ref in ins[1:]:
        value = value + ref[...]
    out[0] = value.T.reshape(out.shape[1:])


def high_rows(part, n):
    return n - 1 if part == "cross" else 1


def send(value, parity, slabs_on, cols_on):
    slabs, n = lax.axis_size("slab"), lax.axis_size("col")
    route = [
        (s * n + c, (s + slabs_on) * n + (c + cols_on) % n)
        for s in range(parity, slabs - slabs_on, 2)
        for c in range(n)
    ]
    return lax.ppermute(value, ("slab", "col"), route)


def shards(green_blocks, traces, sources):
    n = lax.axis_size("col")
    _, _, shots, depth = traces.shape
    lanes = 2 * shots
    trace = ((depth, lanes), f32)
    packing = ((2 * depth, 2 * lanes), bf16)
    rows = min(ROWS, depth // GROUP)

    def copying(part):
        count = (n - 1 if part == "cross" else n) * depth // rows
        return [pltpu.VMEM((count, 2, rows, depth), f32), pltpu.SemaphoreType.DMA((n * depth // rows,))]

    early = ((2, max(depth // AHEAD // rows, 1) * rows, depth), f32)

    def leave(step, chain, part, results):
        by = range(1, n) if part == "cross" else (0,)
        return [send(value, (chain + step) % 2, 1, k) for k, value in zip(by, results)]

    starts = {chain: send(traces, 1 - chain, 1, 0) for chain in (1, 0)}
    green, packs, after, source_t = {}, {}, (), None
    incoming = {(chain, part): [] for chain in (0, 1) for part in ("cross", "own")}
    incoming[0, "own"], incoming[1, "own"] = [starts[0]], [starts[1]]
    for step in range(STEPS):
        last = step == STEPS - 1
        arriving = {}
        for act, chain, part in ORDER[step]:
            if act == "hand":
                for value in incoming[chain, part]:
                    after = tuple(call(hold_kernel, (value,), [((8, lanes), f32)], after=after))
                continue
            cross = part == "cross"
            outs = [trace] * (n - 1 if cross else 1)
            opening = not any(key[0] == chain for key in arriving)
            if act == "open":
                given = [starts[chain]] if cross else [packs[chain], ahead, sources]
                sized = [((high_rows(kind, n) * depth, 2 * depth), bf16) for kind in ("cross", "own") for _ in range(2)]
                first, *results = call(
                    functools.partial(opening_kernel, chain, part, n),
                    given,
                    [packing, early] + sized[:2] + outs if cross else [trace] + sized[2:] + sized[:2] + outs,
                    copying(part),
                    far=(green_blocks,),
                    after=after,
                )
                if cross:
                    ahead, *results = results
                high, low, *results = results
                if cross:
                    packs[chain], green["cross", chain] = first, [high, low]
                else:
                    source_t, green["own"] = first, [high, low]
                    green["cross", 1 - chain], results = results[:2], results[2:]
            else:
                given = green["cross", (chain + step) % 2] if cross else green["own"] + [source_t]
                given = given + (incoming[chain, "cross"] + incoming[chain, "own"] if opening else [packs[chain]])
                results = call(
                    functools.partial(product_kernel, (chain + step) % 2, part, step == 0, None),
                    given,
                    [packing] + outs if opening else outs,
                    after=after,
                )
                if opening:
                    packs[chain], *results = results
            after = (results[-1],)
            arriving[chain, part] = leave(step, chain, part, results)
        if not last:
            incoming = arriving
    given = [value for key in ((1, "cross"), (1, "own"), (0, "cross"), (0, "own")) for value in incoming[key]]
    routes = [[(c, (c + k) % n) for c in range(n)] for k in range(1, n)]
    pieces = max(1, min(PIECES, depth // LANES))
    piece = depth // pieces
    arrived = []
    for i in range(pieces):
        packed, *results = call(
            functools.partial(last_cross_kernel, i),
            green["cross", 0] + green["cross", 1] + given,
            [packing] + [((piece, lanes), f32)] * (n - 1),
            after=after,
        ) if i == 0 else (packed,) + tuple(call(
            functools.partial(last_cross_kernel, i),
            green["cross", 0] + green["cross", 1] + [packed],
            [((piece, lanes), f32)] * (n - 1),
            after=after,
        ))
        after = (results[-1],)
        arrived.append([lax.ppermute(value, "col", route) for value, route in zip(results, routes)])
    (own,) = call(
        functools.partial(product_kernel, None, "own", False, None), green["own"] + [source_t, packed], [trace], after=after
    )
    out = None
    for i in range(pieces):
        ins = [own] + arrived[i]
        out = pl.pallas_call(
            functools.partial(finish_kernel, i, out is not None),
            grid=(1,),
            in_specs=[pl.BlockSpec(memory_space=pltpu.VMEM)] * n + [pl.BlockSpec(memory_space=pl.ANY)] * (out is not None),
            out_specs=pl.BlockSpec((1, 2, shots, piece), functools.partial(lambda i, _: (0, 0, 0, i), i)),
            out_shape=jax.ShapeDtypeStruct(sources.shape, f32),
            input_output_aliases={} if out is None else {n: 0},
            compiler_params=pltpu.CompilerParams(vmem_limit_bytes=VMEM_LIMIT),
        )(*[pinned(a) for a in ins], *([] if out is None else [out]))
    return out


def solution(mesh):
    placed = P("slab", None, None, "col")
    return jax.shard_map(shards, mesh=mesh, in_specs=(placed,) * 3, out_specs=placed, check_vma=False)
```

```python
import functools

import jax
import jax.numpy as jnp
from jax import lax
from jax.experimental import pallas as pl
from jax.experimental.pallas import tpu as pltpu
from jax.sharding import PartitionSpec as P

STEPS = 4
ROWS = 256
GROUP = 1
AHEAD = 4
PIECES = 4
LANES = 128
LAG = 0
ORDER = (
    (("open", 1, "cross"), ("open", 1, "own"), ("make", 0, "cross"), ("make", 0, "own"),),
    (("hand", 1, "cross"), ("make", 1, "cross"), ("hand", 0, "cross"), ("make", 0, "own"), ("make", 1, "own"), ("make", 0, "cross"),),
    (("hand", 1, "cross"), ("hand", 0, "own"), ("hand", 1, "own"), ("make", 1, "cross"), ("make", 1, "own"), ("hand", 0, "cross"), ("make", 0, "cross"), ("make", 0, "own"),),
    (("hand", 1, "cross"), ("hand", 1, "own"), ("hand", 0, "cross"), ("hand", 0, "own"),),
)
VMEM_LIMIT = 24 << 20

f32 = jnp.float32
bf16 = jnp.bfloat16


def in_vmem():
    return pl.BlockSpec(memory_space=pltpu.VMEM)


def pinned(array):
    return pltpu.with_memory_space_constraint(array, pltpu.VMEM)


def call(kernel, args, outs, scratch=(), far=(), after=(), cost=0, **more):
    held = [pltpu.with_memory_space_constraint(a, pltpu.HBM) for a in far] + [pinned(a) for a in args]
    specs = [pl.BlockSpec(memory_space=pltpu.HBM)] * len(far) + [in_vmem()] * len(args)
    first, skip = len(held), len(after)

    def body(*refs):
        kernel(*refs[:first], *refs[first + skip :])

    return pl.pallas_call(
        body,
        in_specs=specs + [pl.BlockSpec(memory_space=pl.ANY)] * skip,
        out_specs=[in_vmem()] * len(outs),
        out_shape=[pltpu.VMEM(shape, dtype) for shape, dtype in outs],
        scratch_shapes=list(scratch),
        compiler_params=pltpu.CompilerParams(vmem_limit_bytes=VMEM_LIMIT),
        cost_estimate=pl.CostEstimate(flops=cost, bytes_accessed=0, transcendentals=0),
        **more,
    )(*held, *after)


def halves(value):
    high = value.astype(bf16)
    return high, (value - high.astype(f32)).astype(bf16)


def hold_kernel(value, out):
    out[...] = jnp.zeros_like(out)


def product(high, low, packed, rows):
    lanes = packed.shape[1] // 2
    both = jnp.dot(high[rows, :], packed[...], preferred_element_type=f32)
    rest = jnp.dot(low[rows, :], packed[:, :lanes], preferred_element_type=f32)
    return both[:, :lanes] + both[:, lanes:] + rest


def active(parity):
    return lax.rem(lax.axis_index("slab"), 2) == parity


def fill(packed, incoming, raw):
    depth, lanes = packed.shape[0] // 2, packed.shape[1] // 2
    if raw:
        value = incoming[0][0].reshape(lanes, depth).T
    else:
        value = incoming[0][...]
        for ref in incoming[1:]:
            value = value + ref[...]
    turned = pltpu.roll(value, lanes // 2, 1)
    lane = lax.broadcasted_iota(jnp.int32, value.shape, 1)
    turned = jnp.where(lane < lanes // 2, -turned, turned)
    packed[:depth, :lanes], packed[:depth, lanes:] = halves(value)
    packed[depth:, :lanes], packed[depth:, lanes:] = halves(turned)


def opening_kernel(parity, part, n, green, *refs):
    buffer, sem = refs[-2:]
    if part == "cross":
        trace, packed, ahead, high, low, *outs = refs[:-2]
    else:
        packed, ahead, source, source_t, high, low, high_cross, low_cross, *outs = refs[:-2]
    step, depth = buffer.shape[2], green.shape[3]
    each = depth // step
    me = lax.axis_index("col")

    def walk(chunks, multiplies, early=0, then=lambda: None):
        def copy(i):
            owner, place = chunks[i][:2]
            first = pl.multiple_of(owner * depth + place * step, step)
            return pltpu.make_async_copy(green.at[0, :, pl.ds(first, step), :], buffer.at[i], sem.at[i])

        def rows(i, half):
            return ahead[half, pl.ds(i * step, step), :] if i < early else buffer[i, half]

        for i in range(early, len(chunks)):
            copy(i).start()
        then()
        if multiplies and part == "cross":
            fill(packed, [trace], True)
        if part == "own":
            source_t[...] = source[0].reshape(-1, depth).T
        lanes = packed.shape[1] // 2
        for j in range(0, len(chunks), GROUP):
            both, rest = None, None
            for i in range(max(j, early), j + GROUP):
                copy(i).wait()
            _, place, (high_to, low_to), to = chunks[j]
            for half in range(2):
                at = (pl.ds(to * step, GROUP * step), pl.ds(half * depth, depth))
                upper, lower = halves(jnp.concatenate([rows(i, half) for i in range(j, j + GROUP)], 0))
                high_to[at], low_to[at] = upper, lower
                if multiplies:
                    weights = packed[pl.ds(half * depth, depth), :]
                    one = jnp.dot(upper, weights, preferred_element_type=f32)
                    two = jnp.dot(lower, weights[:, :lanes], preferred_element_type=f32)
                    both, rest = (one, two) if half == 0 else (both + one, rest + two)
            if multiplies:
                result = both[:, :lanes] + both[:, lanes:] + rest
                inside = pl.ds(place * step, GROUP * step)
                outs[to // each][inside, :] = result if part == "cross" else result + source_t[inside, :]

    def chunks_of(part, to):
        if part == "own":
            return [(me, i, to, i) for i in range(each)]
        return [(lax.rem(me + 1 + k, n), i, to, k * each + i) for k in range(n - 1) for i in range(each)]

    held = ahead.shape[1] // step

    def ahead_copy(i):
        first = pl.multiple_of(me * depth + i * step, step)
        place = ahead.at[:, pl.ds(i * step, step), :]
        return pltpu.make_async_copy(green.at[0, :, pl.ds(first, step), :], place, sem.at[(n - 1) * each + i])

    @pl.when(active(parity))
    def _():
        if part == "cross":
            walk(chunks_of(part, (high, low)), True, then=lambda: [ahead_copy(i).start() for i in range(held)])
            for i in range(held):
                ahead_copy(i).wait()
        else:
            walk(chunks_of(part, (high, low)), True, held)

    if part == "own":

        @pl.when(jnp.logical_not(active(parity)))
        def _():
            walk(chunks_of("cross", (high_cross, low_cross)) + chunks_of("own", (high, low)), False)


def product_kernel(parity, part, raw, piece, high, low, *refs):
    refs = list(refs)
    if part == "own":
        outs, source_t = [refs.pop()], refs.pop(0)
    else:
        count = high.shape[0] // (high.shape[1] // 2)
        refs, outs = refs[:-count], refs[-count:]
    packed = refs.pop()

    def work():
        if refs and not piece:
            fill(packed, refs, raw)
        depth = packed.shape[0] // 2
        if part == "own":
            outs[0][...] = product(high, low, packed, pl.ds(0, depth)) + source_t[...]
        else:
            for k, out in enumerate(outs):
                rows = out.shape[0]
                out[...] = product(high, low, packed, pl.ds(k * depth + (piece or 0) * rows, rows))

    if parity is None:
        work()
    else:
        pl.when(active(parity))(work)


def last_cross_kernel(piece, high_even, low_even, high_odd, low_odd, *refs):
    for parity, high, low in ((0, high_even, low_even), (1, high_odd, low_odd)):
        product_kernel(parity, "cross", False, piece, high, low, *refs)


def finish_kernel(piece, aliased, *refs):
    *ins, out = refs
    if aliased:
        ins = ins[:-1]
    rows = ins[1].shape[0]
    value = ins[0][pl.ds(piece * rows, rows), :]
    for ref in ins[1:]:
        value = value + ref[...]
    out[0] = value.T.reshape(out.shape[1:])


def high_rows(part, n):
    return n - 1 if part == "cross" else 1


def send(value, parity, slabs_on, cols_on):
    slabs, n = lax.axis_size("slab"), lax.axis_size("col")
    route = [
        (s * n + c, (s + slabs_on) * n + (c + cols_on) % n)
        for s in range(parity, slabs - slabs_on, 2)
        for c in range(n)
    ]
    return lax.ppermute(value, ("slab", "col"), route)


def shards(green_blocks, traces, sources):
    n = lax.axis_size("col")
    _, _, shots, depth = traces.shape
    lanes = 2 * shots
    trace = ((depth, lanes), f32)
    packing = ((2 * depth, 2 * lanes), bf16)
    rows = min(ROWS, depth // GROUP)

    def copying(part):
        count = (n - 1 if part == "cross" else n) * depth // rows
        return [pltpu.VMEM((count, 2, rows, depth), f32), pltpu.SemaphoreType.DMA((n * depth // rows,))]

    early = ((2, max(depth // AHEAD // rows, 1) * rows, depth), f32)

    def leave(step, chain, part, results):
        by = range(1, n) if part == "cross" else (0,)
        return [send(value, (chain + step) % 2, 1, k) for k, value in zip(by, results)]

    starts = {chain: send(traces, 1 - chain, 1, 0) for chain in (1, 0)}
    green, packs, after, source_t = {}, {}, (), None
    incoming = {(chain, part): [] for chain in (0, 1) for part in ("cross", "own")}
    incoming[0, "own"], incoming[1, "own"] = [starts[0]], [starts[1]]
    for step in range(STEPS):
        last = step == STEPS - 1
        arriving = {}
        for act, chain, part in ORDER[step]:
            if act == "hand":
                for value in incoming[chain, part]:
                    after = tuple(call(hold_kernel, (value,), [((8, lanes), f32)], after=after))
                continue
            cross = part == "cross"
            outs = [trace] * (n - 1 if cross else 1)
            opening = not any(key[0] == chain for key in arriving)
            if act == "open":
                given = [starts[chain]] if cross else [packs[chain], ahead, sources]
                sized = [((high_rows(kind, n) * depth, 2 * depth), bf16) for kind in ("cross", "own") for _ in range(2)]
                first, *results = call(
                    functools.partial(opening_kernel, chain, part, n),
                    given,
                    [packing, early] + sized[:2] + outs if cross else [trace] + sized[2:] + sized[:2] + outs,
                    copying(part),
                    far=(green_blocks,),
                    after=after,
                )
                if cross:
                    ahead, *results = results
                high, low, *results = results
                if cross:
                    packs[chain], green["cross", chain] = first, [high, low]
                else:
                    source_t, green["own"] = first, [high, low]
                    green["cross", 1 - chain], results = results[:2], results[2:]
            else:
                given = green["cross", (chain + step) % 2] if cross else green["own"] + [source_t]
                given = given + (incoming[chain, "cross"] + incoming[chain, "own"] if opening else [packs[chain]])
                results = call(
                    functools.partial(product_kernel, (chain + step) % 2, part, step == 0, None),
                    given,
                    [packing] + outs if opening else outs,
                    after=after,
                )
                if opening:
                    packs[chain], *results = results
            after = (results[-1],)
            arriving[chain, part] = leave(step, chain, part, results)
        if not last:
            incoming = arriving
    given = [value for key in ((1, "cross"), (1, "own"), (0, "cross"), (0, "own")) for value in incoming[key]]
    routes = [[(c, (c + k) % n) for c in range(n)] for k in range(1, n)]
    pieces = max(1, min(PIECES, depth // LANES))
    piece = depth // pieces
    arrived = []
    for i in range(pieces):
        packed, *results = call(
            functools.partial(last_cross_kernel, i),
            green["cross", 0] + green["cross", 1] + given,
            [packing] + [((piece, lanes), f32)] * (n - 1),
            after=after,
        ) if i == 0 else (packed,) + tuple(call(
            functools.partial(last_cross_kernel, i),
            green["cross", 0] + green["cross", 1] + [packed],
            [((piece, lanes), f32)] * (n - 1),
            after=after,
        ))
        after = (results[-1],)
        arrived.append([lax.ppermute(value, "col", route) for value, route in zip(results, routes)])
    (own,) = call(
        functools.partial(product_kernel, None, "own", False, None), green["own"] + [source_t, packed], [trace], after=after
    )
    out = None
    for i in range(pieces):
        ins = [own] + arrived[i]
        out = pl.pallas_call(
            functools.partial(finish_kernel, i, out is not None),
            grid=(1,),
            in_specs=[pl.BlockSpec(memory_space=pltpu.VMEM)] * n + [pl.BlockSpec(memory_space=pl.ANY)] * (out is not None),
            out_specs=pl.BlockSpec((1, 2, shots, piece), functools.partial(lambda i, _: (0, 0, 0, i), i)),
            out_shape=jax.ShapeDtypeStruct(sources.shape, f32),
            input_output_aliases={} if out is None else {n: 0},
            compiler_params=pltpu.CompilerParams(vmem_limit_bytes=VMEM_LIMIT),
        )(*[pinned(a) for a in ins], *([] if out is None else [out]))
    return out


def solution(mesh):
    placed = P("slab", None, None, "col")
    return jax.shard_map(shards, mesh=mesh, in_specs=(placed,) * 3, out_specs=placed, check_vma=False)
```
